32 devices in a mesh: groups: 2 (over y), dp: 4 (over z), tensor: 4 (over x, core).
Axes of the slice: x: 2, y: 2, z: 4, core: 2. Of those that a mesh axis runs over, the one named last changes fastest.
Arguments:
- kv_cache: bfloat16 [256, 128, 2048], P(('groups', 'dp'), None, 'tensor'), parts along dimension 0
- lengths: int32 [256], P(('groups', 'dp')), parts along dimension 0, may hold values from 1 to 128, as said below
- source: int32 [256], P(('groups', 'dp')), parts along dimension 0, may hold values from 0 to 127, as said below
- queries: bfloat16 [256, 16, 2048], P(('groups', 'dp'), None, 'tensor'), parts along dimension 0, may hold values from -6 to 6
- fresh_kv: bfloat16 [256, 16, 2048], P(('groups', 'dp'), None, 'tensor'), parts along dimension 0, may hold values from -6 to 6
- out_weight: bfloat16 [2048, 4608], P('tensor')
- norm_gain: float32 [4608], P('tensor'), may hold values from 0.5 to 1.5
Outputs:
- normed: bfloat16 [256, 16, 4608], P(('groups', 'dp'), None, 'tensor'), parts along dimension 0
The draws below stay inside these ranges and needn't reach their ends.
There are 2 independent parts, one for each index of `groups`. The reference program is written for one: setup_inputs(seed, part) draws one part's arguments, and reference() takes and returns one part's arrays. A program takes and returns all parts, laid end to end along the dimension named above; an argument that names none is the same for every part. Nothing has to cross between parts.
Inputs may be any that keep to these rules, and one draw needn't show every extreme that they name: `source`: A permutation of the slots. A session may stay on its device or move to another; at most 8 sessions go from one device to any one device, and some device sends 8 to one device. Every device receives 32 sessions, one from each old slot number. `lengths`: some session has 128 cached tokens.
All inputs are finite; a program needn't handle non-finite values.
Results may differ from the reference program's by a relative error of at most 0.018.
Values may be sent and summed in bfloat16 or wider, within the bound.
A program may use at most 64 MiB of HBM per device.

```python
import jax
import jax.numpy as jnp
from jax import lax

D = 4608
HEAD = 128
QHEADS = 16
KVHEADS = 8
S_DEV = 32
CACHE_LEN = 128
BLOCK_ROWS = 16
SESSIONS = 128
N_TENSOR = 4


def draw_source(key, part):
    dp_count = SESSIONS // S_DEV
    key_place, key_offset, key_slots = jax.random.split(jax.random.fold_in(key, 11), 3)
    placing = jax.random.permutation(key_place, dp_count).astype(jnp.int32)
    offsets = jax.random.permutation(key_offset, dp_count).astype(jnp.int32)[jnp.arange(S_DEV) % dp_count]
    new_home = (placing[:, None] + offsets[None, :]) % dp_count
    orders = jax.vmap(lambda sub_key: jax.random.permutation(sub_key, S_DEV))(jax.random.split(key_slots, dp_count)).astype(jnp.int32)
    slot_ids = jnp.arange(S_DEV, dtype=jnp.int32)
    new_slot = orders[new_home, slot_ids[None, :]]
    new_global = (new_home * S_DEV + new_slot).reshape(-1)
    old_global = jnp.arange(SESSIONS, dtype=jnp.int32)
    return jnp.zeros((SESSIONS,), jnp.int32).at[new_global].set(old_global)


def draw_lengths(key, part):
    dp_count = SESSIONS // S_DEV
    key_heavy, key_value, key_spot = jax.random.split(jax.random.fold_in(key, 23), 3)
    heavy_dev = jax.random.randint(key_heavy, (dp_count, 1), 0, 2)
    lowest = jnp.where(heavy_dev == 1, CACHE_LEN // 2, 1)
    highest = jnp.where(heavy_dev == 1, CACHE_LEN, max(CACHE_LEN // 4, 1))
    spread = jax.random.randint(key_value, (dp_count, S_DEV), 0, 1 << 20)
    drawn = (lowest + spread % (highest - lowest + 1)).reshape(-1)
    full_spot = jax.random.randint(key_spot, (), 0, SESSIONS)
    return jnp.where(jnp.arange(SESSIONS) == full_spot, CACHE_LEN, drawn).astype(jnp.int32)


def base_values(key, shape):
    return jax.random.truncated_normal(key, -6.0, 6.0, shape, jnp.float32)


def draw_out_weight(key, part):
    row_total = QHEADS * HEAD
    row_block = row_total // 8
    col_block = D // 8
    key_base, key_grid, key_cols = jax.random.split(jax.random.fold_in(key, 37), 3)
    base = base_values(key_base, (row_total, D))
    grid_log = jax.random.uniform(key_grid, (8, 8), jnp.float32, -1.2, 1.2)
    column_log = jax.random.uniform(key_cols, (1, 8), jnp.float32, -0.7, 0.7)
    block_scale = jnp.exp(grid_log + column_log)
    block_scale = jnp.repeat(jnp.repeat(block_scale, row_block, axis=0), col_block, axis=1)
    return (base * block_scale * (0.57 * row_total ** (-0.5))).astype(jnp.bfloat16)


def draw_kv_cache(key, part):
    key_base, key_scale = jax.random.split(jax.random.fold_in(key, 41), 2)
    base = base_values(key_base, (SESSIONS, CACHE_LEN, KVHEADS, 2, HEAD))
    value_log = jax.random.uniform(key_scale, (SESSIONS, 1, KVHEADS, 1, 1), jnp.float32, -1.2, 1.2)
    key_part = jnp.ones((SESSIONS, 1, KVHEADS, 1, 1), jnp.float32)
    half_scale = jnp.concatenate([key_part, jnp.exp(value_log)], axis=3)
    scaled = base * half_scale
    return scaled.reshape(SESSIONS, CACHE_LEN, KVHEADS * 2 * HEAD).astype(jnp.bfloat16)


def levels(stream_key, dims, pieces, least, high):
    def one(axis_at, parts):
        heights = jax.random.uniform(jax.random.fold_in(jax.random.fold_in(stream_key, 6), axis_at), (parts,), jnp.float32, least / len(pieces), high / len(pieces))
        return jnp.repeat(jnp.exp(heights), dims[axis_at] // parts).reshape((-1,) + (1,) * (len(dims) - axis_at - 1))

    loudness = one(*pieces[0])
    for cut in pieces[1:]:
        loudness = loudness * one(*cut)
    return loudness


def noise(own_key, dims, width, most, cuts=(), held_as=jnp.bfloat16):
    entries = width * jax.random.normal(own_key, dims, jnp.float32)
    if cuts:
        entries = entries * levels(own_key, dims, cuts, -0.22, 0.18)
    return jnp.clip(entries, -most, most).astype(held_as)


def setup_inputs(seed: int = 0, part: int = 0) -> dict:
    arg_keys = jax.random.split(jax.random.key(seed), 8)
    own_keys = jax.random.split(jax.random.fold_in(arg_keys[7], part), 8)
    kv_cache = draw_kv_cache(jax.random.fold_in(jax.random.fold_in(arg_keys[7], part), 71), part)
    lengths = draw_lengths(jax.random.fold_in(jax.random.fold_in(arg_keys[7], part), 71), part)
    source = draw_source(jax.random.fold_in(jax.random.fold_in(arg_keys[7], part), 71), part)
    queries = noise(own_keys[3], (SESSIONS, BLOCK_ROWS, QHEADS * HEAD), 1.0, 6.0, ((0, 4), (2, 4)))
    fresh_kv = noise(own_keys[4], (SESSIONS, BLOCK_ROWS, KVHEADS * 2 * HEAD), 1.0, 6.0, ((0, 4), (2, 4)))
    out_weight = draw_out_weight(jax.random.fold_in(arg_keys[7], 71), part)
    norm_gain = jnp.clip(1.0 + 0.1 * jax.random.normal(arg_keys[6], (D,), jnp.float32), 0.5, 1.5)
    return {"kv_cache": kv_cache, "lengths": lengths, "source": source, "queries": queries, "fresh_kv": fresh_kv, "out_weight": out_weight, "norm_gain": norm_gain}


score_scale = 144.0 ** (-0.5)
soft_cap = 50.0
norm_eps = 1e-06

def rounded_copy(values):
    return lax.optimization_barrier(values.astype(jnp.bfloat16)).astype(jnp.float32)

def attend_slot(queries, cached, length, fresh_kv):
    cache_length = cached.shape[0]
    row_count = queries.shape[0]
    group_size = QHEADS // KVHEADS
    key_values = jnp.concatenate([cached, fresh_kv], axis=0).astype(jnp.float32)
    key_values = key_values.reshape(cache_length + row_count, KVHEADS, 2, HEAD)
    key_rows = key_values[:, :, 0]
    value_rows = key_values[:, :, 1]
    grouped = queries.astype(jnp.float32).reshape(row_count, KVHEADS, group_size, HEAD)
    scores = jnp.einsum('rkgh,jkh->kgrj', grouped, key_rows) * score_scale
    capped = soft_cap * jnp.tanh(scores / soft_cap)
    position = jnp.arange(cache_length + row_count, dtype=jnp.int32)
    row_position = jnp.arange(row_count, dtype=jnp.int32)
    in_cache = position[None, :] < length
    in_block = (position[None, :] >= cache_length) & (position[None, :] - cache_length <= row_position[:, None])
    visible = in_cache | in_block
    weights = jnp.where(visible[None, None], jnp.exp(capped), 0.0)
    soft_weights = rounded_copy(weights / lax.optimization_barrier(jnp.sum(weights, axis=-1, keepdims=True)))
    attended = jnp.einsum('kgrj,jkh->rkgh', soft_weights, value_rows)
    return attended.reshape(row_count, QHEADS * HEAD).astype(jnp.bfloat16)

def reference(kv_cache, lengths, source, queries, fresh_kv, out_weight, norm_gain):

    def per_slot(session_index):
        anchor = source[session_index]
        return attend_slot(queries[session_index], kv_cache[anchor], lengths[anchor], fresh_kv[session_index])
    attended = lax.map(per_slot, jnp.arange(SESSIONS, dtype=jnp.int32))
    flat_rows = attended.reshape(SESSIONS * BLOCK_ROWS, QHEADS * HEAD)
    head_cols = QHEADS * HEAD // N_TENSOR
    branch = jnp.zeros((flat_rows.shape[0], D), jnp.float32)
    for shard_index in range(N_TENSOR):
        partial_value = jnp.dot(flat_rows[:, shard_index * head_cols:(shard_index + 1) * head_cols], out_weight[shard_index * head_cols:(shard_index + 1) * head_cols], preferred_element_type=jnp.float32)
        branch = branch + rounded_copy(partial_value)
    mean_square = lax.optimization_barrier(jnp.mean(branch * branch, axis=-1, keepdims=True))
    normed = branch * lax.rsqrt(mean_square + norm_eps) * norm_gain
    return normed.astype(jnp.bfloat16).reshape(SESSIONS, BLOCK_ROWS, D)
```

```python
import functools

import jax
import jax.numpy as jnp
from jax import lax
from jax.experimental import pallas as pl
from jax.experimental.pallas import tpu as pltpu
from jax.sharding import PartitionSpec as P

HEAD = 128
QHEADS = 16
KVHEADS = 8
GROUP = QHEADS // KVHEADS

score_scale = 144.0 ** (-0.5)
soft_cap = 50.0
norm_eps = 1e-06

MESH = pl.DeviceIdType.MESH
NT = (((1,), (1,)), ((), ()))


def capped_exp(scores):
    return jnp.exp(soft_cap * jnp.tanh(scores * (score_scale / soft_cap)))


def kernel(
    dp_count,
    tensor_count,
    cap,
    model_width,
    lengths,
    slot_of_lane,
    lane_of_slot,
    old_slot_of_lane,
    old_slots,
    gain,
    kv_hbm,
    q_hbm,
    fresh_hbm,
    w_hbm,
    out,
    kv,
    q,
    fresh,
    w,
    ql,
    fl,
    q_in,
    idx_in,
    idx_smem,
    res_out,
    res_in,
    den_out,
    den_in,
    fresh_acc,
    att,
    part_out,
    part_in,
    branch,
    ss_out,
    ss_in,
    local_sem,
    w_send,
    w_recv,
    q_send,
    q_recv,
    i_send,
    i_recv,
    s_sem,
    r_send,
    r_recv,
    d_send,
    d_recv,
    a_send,
    a_recv,
    p_send,
    p_recv,
    n_send,
    n_recv,
):
    slots, rows, q_width = q.shape
    cache_len = kv.shape[1]
    kv_heads = kv.shape[2] // (2 * HEAD)
    q_heads = q_width // HEAD
    halves = tensor_count // 2
    own_cols = out.shape[2]
    chunks, chunk_rows, _ = att.shape
    chunk_lanes = slots // chunks
    per_chunk = chunk_lanes // cap
    depth = w_hbm.shape[-2]

    me = lax.axis_index("dp")
    my_t = lax.axis_index("tensor")
    partner = my_t + 1 - 2 * lax.rem(my_t, 2)

    def dp_peer(o):
        return lax.rem(me + o, dp_count)

    def t_peer(u):
        return lax.rem(my_t + u, tensor_count)

    def w_block(block):
        if len(w_hbm.shape) == 3:
            return w_hbm.at[block]
        return w_hbm.at[:, pl.ds(pl.multiple_of(block * own_cols, 128), own_cols)]

    load_q = pltpu.make_async_copy(q_hbm, q, local_sem.at[0])
    load_fresh = pltpu.make_async_copy(fresh_hbm, fresh, local_sem.at[1])
    load_kv = pltpu.make_async_copy(kv_hbm, kv, local_sem.at[2])
    load_w = [
        pltpu.make_async_copy(
            w_block(t_peer(2 * m)), w.at[m, pl.ds(0, depth)], local_sem.at[3 + m]
        )
        for m in range(halves)
    ]
    load_q.start()
    load_fresh.start()
    load_kv.start()
    for m in range(halves):
        load_w[m].start()

    barrier = pltpu.get_barrier_semaphore()
    for o in range(1, dp_count):
        pl.semaphore_signal(barrier, 1, device_id={"dp": dp_peer(o)}, device_id_type=MESH)
    for u in range(1, tensor_count):
        pl.semaphore_signal(barrier, 1, device_id={"tensor": t_peer(u)}, device_id_type=MESH)
    pl.semaphore_wait(barrier, dp_count - 1 + tensor_count - 1)

    def remote(src, dst, send, recv, where):
        return pltpu.make_async_remote_copy(
            src_ref=src, dst_ref=dst, send_sem=send, recv_sem=recv, device_id=where, device_id_type=MESH
        )

    send_w = [
        remote(
            w_block(lax.rem(partner + 2 * m, tensor_count)),
            w.at[m, pl.ds(depth, depth)],
            w_send.at[m],
            w_recv.at[m],
            {"tensor": partner},
        )
        for m in range(halves)
    ]
    send_q, send_i, send_r, send_d = {}, {}, {}, {}
    for o in range(1, dp_count):
        lanes = pl.ds(o * cap, cap)
        there, back = {"dp": dp_peer(o)}, {"dp": dp_peer(dp_count - o)}
        send_q[o] = remote(ql.at[lanes], q_in.at[lanes], q_send.at[o], q_recv.at[o], there)
        send_i[o] = remote(old_slots.at[o], idx_in.at[o], i_send.at[o], i_recv.at[o], there)
        send_r[o] = remote(res_out.at[lanes], res_in.at[lanes], r_send.at[o], r_recv.at[o], back)
        send_d[o] = remote(den_out.at[o], den_in.at[o], d_send.at[o], d_recv.at[o], back)
    send_a = [
        remote(
            att.at[c, :, pl.ds(0, q_width)],
            att.at[c, :, pl.ds(q_width, q_width)],
            a_send.at[c],
            a_recv.at[c],
            {"tensor": partner},
        )
        for c in range(chunks)
    ]
    send_p = {
        (c, m): remote(
            part_out.at[c, m], part_in.at[c, m], p_send.at[c, m], p_recv.at[c, m], {"tensor": t_peer(2 * m)}
        )
        for c in range(chunks)
        for m in range(1, halves)
    }
    send_n = {
        (c, u): remote(ss_out.at[c], ss_in.at[c, u], n_send.at[c, u], n_recv.at[c, u], {"tensor": t_peer(u)})
        for c in range(chunks)
        for u in range(1, tensor_count)
    }

    load_q.wait()

    def to_lane(lane, _):
        ql[lane] = q[slot_of_lane[lane]]
        return 0

    lax.fori_loop(0, slots, to_lane, 0, unroll=8)
    for o in range(1, dp_count):
        send_i[o].start()
        send_q[o].start()
    for m in range(halves - 1, -1, -1):
        send_w[m].start()
    load_fresh.wait()

    def fresh_to_lane(lane, _):
        fl[lane] = fresh[slot_of_lane[lane]]
        return 0

    lax.fori_loop(0, slots, fresh_to_lane, 0, unroll=8)
    load_kv.wait()

    column = lax.broadcasted_iota(jnp.int32, (rows, HEAD), 1)
    position = lax.broadcasted_iota(jnp.int32, (GROUP * rows, cache_len), 1)
    ones = jnp.ones((cache_len, HEAD), jnp.bfloat16)

    def serve(q_ref, o, slot_at, res, dens):
        total = jnp.zeros((rows, HEAD), jnp.float32)
        for k in range(cap):
            lane = o * cap + k
            slot = slot_at(k)
            length = lengths[slot]
            for h in range(kv_heads):
                first = GROUP * h * HEAD
                asked = jnp.concatenate(
                    [q_ref[lane, :, first + g * HEAD : first + (g + 1) * HEAD] for g in range(GROUP)], axis=0
                )
                keys = kv[slot, :, 2 * h * HEAD : (2 * h + 1) * HEAD]
                values = kv[slot, :, (2 * h + 1) * HEAD : (2 * h + 2) * HEAD]
                scores = lax.dot_general(asked, keys, NT, preferred_element_type=jnp.float32)
                weights = jnp.where(position < length, capped_exp(scores), 0.0).astype(jnp.bfloat16)
                summed = jnp.dot(
                    weights, jnp.concatenate([values, ones], axis=1), preferred_element_type=jnp.float32
                )
                for g in range(GROUP):
                    part = summed[g * rows : (g + 1) * rows]
                    res[lane, :, first + g * HEAD : first + (g + 1) * HEAD] = part[:, :HEAD].astype(jnp.bfloat16)
                    total = jnp.where(column == k * q_heads + GROUP * h + g, part[:, HEAD:], total)
        dens[o] = total

    chunk_keys = chunk_lanes * rows
    row_id = lax.rem(lax.broadcasted_iota(jnp.int32, (GROUP * chunk_keys, chunk_keys), 0), chunk_keys)
    key_id = lax.broadcasted_iota(jnp.int32, (GROUP * chunk_keys, chunk_keys), 1)
    in_block = (row_id // rows == key_id // rows) & (key_id <= row_id)
    fresh_ones = jnp.ones((chunk_keys, HEAD), jnp.bfloat16)

    def fresh_part(c):
        lanes = slice(c * chunk_lanes, (c + 1) * chunk_lanes)
        for h in range(kv_heads):
            first = GROUP * h * HEAD
            asked = jnp.concatenate(
                [
                    ql[lanes, :, first + g * HEAD : first + (g + 1) * HEAD].reshape(chunk_keys, HEAD)
                    for g in range(GROUP)
                ],
                axis=0,
            )
            keys = fl[lanes, :, 2 * h * HEAD : (2 * h + 1) * HEAD].reshape(chunk_keys, HEAD)
            values = fl[lanes, :, (2 * h + 1) * HEAD : (2 * h + 2) * HEAD].reshape(chunk_keys, HEAD)
            scores = lax.dot_general(asked, keys, NT, preferred_element_type=jnp.float32)
            weights = jnp.where(in_block, capped_exp(scores), 0.0).astype(jnp.bfloat16)
            fresh_acc[c, h] = jnp.dot(
                weights, jnp.concatenate([values, fresh_ones], axis=1), preferred_element_type=jnp.float32
            )

    def combine(c):
        for o in range(c * per_chunk, (c + 1) * per_chunk):
            if o:
                send_r[o].wait_recv()
                send_d[o].wait_recv()
        for i in range(chunk_lanes):
            lane = c * chunk_lanes + i
            o, k = lane // cap, lane % cap
            for h in range(kv_heads):
                for g in range(GROUP):
                    head = GROUP * h + g
                    at = slice(g * chunk_keys + i * rows, g * chunk_keys + (i + 1) * rows)
                    cols = slice(head * HEAD, (head + 1) * HEAD)
                    place = k * q_heads + head
                    den = fresh_acc[c, h, at, HEAD:] + den_in[o, :, place : place + 1]
                    num = fresh_acc[c, h, at, :HEAD] + res_in[lane, :, cols].astype(jnp.float32)
                    att[c, i * rows : (i + 1) * rows, cols] = (num / den).astype(jnp.bfloat16)
        send_a[c].start()

    def project(c):
        send_a[c].wait_recv()
        if c == 0:
            for m in range(halves):
                load_w[m].wait()
                send_w[m].wait_recv()
        for m in range(1, halves):
            part_out[c, m] = jnp.dot(att[c], w[m], preferred_element_type=jnp.float32).astype(jnp.bfloat16)
            send_p[c, m].start()
        own = jnp.dot(att[c], w[0], preferred_element_type=jnp.float32)
        branch[c * chunk_lanes : (c + 1) * chunk_lanes] = own.reshape(chunk_lanes, rows, own_cols)

    def gather_sum(c):
        here = slice(c * chunk_lanes, (c + 1) * chunk_lanes)
        total = branch[here].reshape(chunk_rows, own_cols)
        for m in range(1, halves):
            send_p[c, m].wait_recv()
            total = total + part_in[c, m].astype(jnp.float32)
        branch[here] = total.reshape(chunk_lanes, rows, own_cols)
        squares = jnp.sum(total * total, axis=1, keepdims=True)
        ss_out[c] = jnp.transpose(jnp.broadcast_to(squares, (chunk_rows, chunk_rows)))[:8]
        for u in range(1, tensor_count):
            send_n[c, u].start()

    serve(ql, 0, lambda k: old_slot_of_lane[k], res_in, den_in)
    fresh_part(0)
    if per_chunk == 1:
        combine(0)
    for c in range(1, chunks):
        fresh_part(c)
    if per_chunk == 1:
        project(0)
    for o in range(1, dp_count):
        send_i[o].wait_recv()
        spill = pltpu.make_async_copy(idx_in.at[o], idx_smem.at[o], s_sem.at[o])
        spill.start()
        spill.wait()
        send_q[o].wait_recv()
        serve(q_in, o, lambda k, o=o: idx_smem[o, 0, k], res_out, den_out)
        send_d[o].start()
        send_r[o].start()
    for c in range(chunks):
        if c or per_chunk > 1:
            combine(c)
            project(c)
        if c:
            gather_sum(c - 1)
    gather_sum(chunks - 1)

    for c in range(chunks):
        squares = ss_out[c]
        for u in range(1, tensor_count):
            send_n[c, u].wait_recv()
            squares = squares + ss_in[c, u]
        wide = jnp.broadcast_to(squares[:1], (chunk_rows, chunk_rows))
        mean_square = jnp.transpose(wide)[:, :1] * (1.0 / model_width)
        here = slice(c * chunk_lanes, (c + 1) * chunk_lanes)
        scale = lax.rsqrt(mean_square + norm_eps)
        normed = branch[here].reshape(chunk_rows, own_cols) * scale * gain[...]
        branch[here] = normed.reshape(chunk_lanes, rows, own_cols)

    def to_slot(slot, _):
        out[slot] = branch[lane_of_slot[slot]].astype(jnp.bfloat16)
        return 0

    lax.fori_loop(0, slots, to_slot, 0, unroll=4)

    for o in range(1, dp_count):
        for sent in (send_q[o], send_i[o], send_r[o], send_d[o]):
            sent.wait_send()
    for sent in [*send_w, *send_a, *send_p.values(), *send_n.values()]:
        sent.wait_send()


def shards(kv_cache, lengths, source, queries, fresh_kv, out_weight, norm_gain):
    dp_count = lax.axis_size("dp")
    tensor_count = lax.axis_size("tensor")
    slots, rows, q_width = queries.shape
    kv_width = kv_cache.shape[2]
    kv_heads = kv_width // (2 * HEAD)
    cap = max(1, slots // dp_count)
    model_width = out_weight.shape[1]
    true_cols = norm_gain.shape[0]
    own_cols = -(-true_cols // 128) * 128
    depth = out_weight.shape[0]
    halves = tensor_count // 2
    chunk_lanes = max(cap, slots // 4)
    chunks = slots // chunk_lanes
    chunk_rows = chunk_lanes * rows

    if own_cols != true_cols:
        spare = own_cols - true_cols
        blocks = out_weight.reshape(depth, tensor_count, true_cols).transpose(1, 0, 2)
        out_weight = jnp.pad(blocks, ((0, 0), (0, 0), (0, spare)))
        norm_gain = jnp.pad(norm_gain, (0, spare))

    home = source // slots
    offset = (home - lax.axis_index("dp").astype(jnp.int32) + dp_count) % dp_count
    ids = jnp.arange(slots, dtype=jnp.int32)
    same = (offset[:, None] == offset[None, :]) & (ids[None, :] < ids[:, None])
    lane_of_slot = offset * cap + jnp.sum(same.astype(jnp.int32), axis=1)
    hits = lane_of_slot[None, :] == ids[:, None]
    slot_of_lane = jnp.sum(jnp.where(hits, ids[None, :], 0), axis=1)
    old_slot = jnp.sum(jnp.where(hits, (source % slots)[None, :], 0), axis=1)
    old_slots = jnp.pad(old_slot.reshape(dp_count, 1, cap), ((0, 0), (0, 7), (0, 128 - cap)))

    vmem = pl.BlockSpec(memory_space=pltpu.VMEM)
    smem = pl.BlockSpec(memory_space=pltpu.SMEM)
    hbm = pl.BlockSpec(memory_space=pl.ANY)
    dma = pltpu.SemaphoreType.DMA
    bf16, f32, i32 = jnp.bfloat16, jnp.float32, jnp.int32
    normed = pl.pallas_call(
        functools.partial(kernel, dp_count, tensor_count, cap, model_width),
        out_shape=jax.ShapeDtypeStruct((slots, rows, own_cols), bf16),
        in_specs=[smem, smem, smem, smem, vmem, vmem, hbm, hbm, hbm, hbm],
        out_specs=vmem,
        scratch_shapes=[
            pltpu.VMEM(kv_cache.shape, bf16),
            pltpu.VMEM(queries.shape, bf16),
            pltpu.VMEM(fresh_kv.shape, bf16),
            pltpu.VMEM((halves, 2 * depth, own_cols), bf16),
            pltpu.VMEM(queries.shape, bf16),
            pltpu.VMEM(fresh_kv.shape, bf16),
            pltpu.VMEM(queries.shape, bf16),
            pltpu.VMEM((dp_count, 8, 128), i32),
            pltpu.SMEM((dp_count, 8, 128), i32),
            pltpu.VMEM(queries.shape, bf16),
            pltpu.VMEM(queries.shape, bf16),
            pltpu.VMEM((dp_count, rows, 128), f32),
            pltpu.VMEM((dp_count, rows, 128), f32),
            pltpu.VMEM((chunks, kv_heads, GROUP * chunk_rows, 2 * HEAD), f32),
            pltpu.VMEM((chunks, chunk_rows, 2 * q_width), bf16),
            pltpu.VMEM((chunks, halves, chunk_rows, own_cols), bf16),
            pltpu.VMEM((chunks, halves, chunk_rows, own_cols), bf16),
            pltpu.VMEM((slots, rows, own_cols), f32),
            pltpu.VMEM((chunks, 8, 128), f32),
            pltpu.VMEM((chunks, tensor_count, 8, 128), f32),
            dma((3 + halves,)),
            dma((halves,)),
            dma((halves,)),
            *[dma((dp_count,)) for _ in range(9)],
            dma((chunks,)),
            dma((chunks,)),
            dma((chunks, halves)),
            dma((chunks, halves)),
            dma((chunks, tensor_count)),
            dma((chunks, tensor_count)),
        ],
        compiler_params=pltpu.CompilerParams(
            collective_id=0, has_side_effects=True, vmem_limit_bytes=48 * 2**20
        ),
        cost_estimate=pl.CostEstimate(
            flops=2 * slots * rows * depth * own_cols * tensor_count,
            bytes_accessed=2 * (kv_cache.size + out_weight.size),
            transcendentals=0,
        ),
    )(
        lengths,
        slot_of_lane,
        lane_of_slot,
        old_slot,
        old_slots,
        norm_gain.reshape(1, own_cols),
        kv_cache,
        queries,
        fresh_kv,
        out_weight,
    )
    return normed[:, :, :true_cols]


def solution(mesh):
    placed = (
        P(("groups", "dp"), None, "tensor"),
        P(("groups", "dp")),
        P(("groups", "dp")),
        P(("groups", "dp"), None, "tensor"),
        P(("groups", "dp"), None, "tensor"),
        P("tensor", None),
        P("tensor"),
    )
    return jax.shard_map(
        shards,
        mesh=mesh,
        in_specs=placed,
        out_specs=P(("groups", "dp"), None, "tensor"),
        check_vma=False,
    )
```

```python
import functools

import jax
import jax.numpy as jnp
from jax import lax
from jax.experimental import pallas as pl
from jax.experimental.pallas import tpu as pltpu
from jax.sharding import PartitionSpec as P

HEAD = 128
QHEADS = 16
KVHEADS = 8
GROUP = QHEADS // KVHEADS

score_scale = 144.0 ** (-0.5)
soft_cap = 50.0
norm_eps = 1e-06

MESH = pl.DeviceIdType.MESH
NT = (((1,), (1,)), ((), ()))


def capped_exp(scores):
    return jnp.exp(soft_cap * jnp.tanh(scores * (score_scale / soft_cap)))


def kernel(
    dp_count,
    tensor_count,
    cap,
    model_width,
    old_slots,
    gain,
    lists_hbm,
    kv_hbm,
    q_hbm,
    fresh_hbm,
    w_hbm,
    out,
    kv,
    q,
    fresh,
    w,
    ql,
    fl,
    q_in,
    idx_in,
    idx_smem,
    lists,
    res_out,
    res_in,
    den_out,
    den_in,
    fresh_acc,
    att,
    part_out,
    part_in,
    branch,
    ss_out,
    ss_in,
    local_sem,
    w_send,
    w_recv,
    q_send,
    q_recv,
    i_send,
    i_recv,
    s_sem,
    r_send,
    r_recv,
    d_send,
    d_recv,
    a_send,
    a_recv,
    p_send,
    p_recv,
    n_send,
    n_recv,
):
    slots, rows, q_width = q.shape
    cache_len = kv.shape[1]
    kv_heads = kv.shape[2] // (2 * HEAD)
    q_heads = q_width // HEAD
    halves = tensor_count // 2
    own_cols = out.shape[2]
    chunks, chunk_rows, _ = att.shape
    chunk_lanes = slots // chunks
    per_chunk = chunk_lanes // cap
    depth = w_hbm.shape[-2]

    me = lax.axis_index("dp")
    my_t = lax.axis_index("tensor")
    partner = my_t + 1 - 2 * lax.rem(my_t, 2)

    def dp_peer(o):
        return lax.rem(me + o, dp_count)

    def t_peer(u):
        return lax.rem(my_t + u, tensor_count)

    def w_block(block):
        if len(w_hbm.shape) == 3:
            return w_hbm.at[block]
        return w_hbm.at[:, pl.ds(pl.multiple_of(block * own_cols, 128), own_cols)]

    def length_of(slot):
        return lists[slot]

    def slot_of(lane):
        return lists[slots + lane]

    def lane_of(slot):
        return lists[2 * slots + slot]

    load_lists = pltpu.make_async_copy(lists_hbm, lists, s_sem.at[0])
    load_q = pltpu.make_async_copy(q_hbm, q, local_sem.at[0])
    load_fresh = pltpu.make_async_copy(fresh_hbm, fresh, local_sem.at[1])
    load_kv = pltpu.make_async_copy(kv_hbm, kv, local_sem.at[2])
    load_w = [
        pltpu.make_async_copy(
            w_block(t_peer(2 * m)), w.at[m, pl.ds(0, depth)], local_sem.at[3 + m]
        )
        for m in range(halves)
    ]
    load_lists.start()
    load_q.start()
    load_kv.start()
    load_fresh.start()
    for m in range(halves - 1, -1, -1):
        load_w[m].start()

    barrier = pltpu.get_barrier_semaphore()
    for o in range(1, dp_count):
        pl.semaphore_signal(barrier, 1, device_id={"dp": dp_peer(o)}, device_id_type=MESH)
    for u in range(1, tensor_count):
        pl.semaphore_signal(barrier, 1, device_id={"tensor": t_peer(u)}, device_id_type=MESH)
    load_lists.wait()
    load_q.wait()

    def to_lane(lane, _):
        ql[lane] = q[slot_of(lane)]
        return 0

    lax.fori_loop(0, slots, to_lane, 0, unroll=8)
    pl.semaphore_wait(barrier, dp_count - 1 + tensor_count - 1)

    def remote(src, dst, send, recv, where):
        return pltpu.make_async_remote_copy(
            src_ref=src, dst_ref=dst, send_sem=send, recv_sem=recv, device_id=where, device_id_type=MESH
        )

    send_w = [
        remote(
            w_block(lax.rem(partner + 2 * m, tensor_count)),
            w.at[m, pl.ds(depth, depth)],
            w_send.at[m],
            w_recv.at[m],
            {"tensor": partner},
        )
        for m in range(halves)
    ]
    send_q, send_i, send_r, send_d = {}, {}, {}, {}
    for o in range(1, dp_count):
        lanes = pl.ds(o * cap, cap)
        there, back = {"dp": dp_peer(o)}, {"dp": dp_peer(dp_count - o)}
        send_q[o] = remote(ql.at[lanes], q_in.at[lanes], q_send.at[o], q_recv.at[o], there)
        send_i[o] = remote(old_slots.at[o], idx_in.at[o], i_send.at[o], i_recv.at[o], there)
        send_r[o] = remote(res_out.at[lanes], res_in.at[lanes], r_send.at[o], r_recv.at[o], back)
        send_d[o] = remote(den_out.at[o], den_in.at[o], d_send.at[o], d_recv.at[o], back)
    send_a = [
        remote(
            att.at[c, :, pl.ds(0, q_width)],
            att.at[c, :, pl.ds(q_width, q_width)],
            a_send.at[c],
            a_recv.at[c],
            {"tensor": partner},
        )
        for c in range(chunks)
    ]
    send_p = {
        (c, m): remote(
            part_out.at[c, m], part_in.at[c, m], p_send.at[c, m], p_recv.at[c, m], {"tensor": t_peer(2 * m)}
        )
        for c in range(chunks)
        for m in range(1, halves)
    }
    send_n = {
        (c, u): remote(ss_out.at[c], ss_in.at[c, u], n_send.at[c, u], n_recv.at[c, u], {"tensor": t_peer(u)})
        for c in range(chunks)
        for u in range(1, tensor_count)
    }

    for o in range(1, dp_count):
        send_i[o].start()
        send_q[o].start()
    for m in range(halves - 1, -1, -1):
        send_w[m].start()
    load_fresh.wait()

    def fresh_to_lane(lane, _):
        fl[lane] = fresh[slot_of(lane)]
        return 0

    lax.fori_loop(0, slots, fresh_to_lane, 0, unroll=8)
    load_kv.wait()

    column = lax.broadcasted_iota(jnp.int32, (rows, HEAD), 1)
    position = lax.broadcasted_iota(jnp.int32, (GROUP * rows, cache_len), 1)
    ones = jnp.ones((cache_len, HEAD), jnp.bfloat16)

    def serve(q_ref, o, slot_at, res, dens):
        total = jnp.zeros((rows, HEAD), jnp.float32)
        for k in range(cap):
            lane = o * cap + k
            slot = slot_at(k)
            length = length_of(slot)
            for h in range(kv_heads):
                first = GROUP * h * HEAD
                asked = jnp.concatenate(
                    [q_ref[lane, :, first + g * HEAD : first + (g + 1) * HEAD] for g in range(GROUP)], axis=0
                )
                keys = kv[slot, :, 2 * h * HEAD : (2 * h + 1) * HEAD]
                values = kv[slot, :, (2 * h + 1) * HEAD : (2 * h + 2) * HEAD]
                scores = lax.dot_general(asked, keys, NT, preferred_element_type=jnp.float32)
                weights = jnp.where(position < length, capped_exp(scores), 0.0).astype(jnp.bfloat16)
                summed = jnp.dot(
                    weights, jnp.concatenate([values, ones], axis=1), preferred_element_type=jnp.float32
                )
                for g in range(GROUP):
                    part = summed[g * rows : (g + 1) * rows]
                    res[lane, :, first + g * HEAD : first + (g + 1) * HEAD] = part[:, :HEAD].astype(jnp.bfloat16)
                    total = jnp.where(column == k * q_heads + GROUP * h + g, part[:, HEAD:], total)
        dens[o] = total

    chunk_keys = chunk_lanes * rows
    row_id = lax.rem(lax.broadcasted_iota(jnp.int32, (GROUP * chunk_keys, chunk_keys), 0), chunk_keys)
    key_id = lax.broadcasted_iota(jnp.int32, (GROUP * chunk_keys, chunk_keys), 1)
    in_block = (row_id // rows == key_id // rows) & (key_id <= row_id)
    fresh_ones = jnp.ones((chunk_keys, HEAD), jnp.bfloat16)

    def fresh_part(c):
        lanes = slice(c * chunk_lanes, (c + 1) * chunk_lanes)
        for h in range(kv_heads):
            first = GROUP * h * HEAD
            asked = jnp.concatenate(
                [
                    ql[lanes, :, first + g * HEAD : first + (g + 1) * HEAD].reshape(chunk_keys, HEAD)
                    for g in range(GROUP)
                ],
                axis=0,
            )
            keys = fl[lanes, :, 2 * h * HEAD : (2 * h + 1) * HEAD].reshape(chunk_keys, HEAD)
            values = fl[lanes, :, (2 * h + 1) * HEAD : (2 * h + 2) * HEAD].reshape(chunk_keys, HEAD)
            scores = lax.dot_general(asked, keys, NT, preferred_element_type=jnp.float32)
            weights = jnp.where(in_block, capped_exp(scores), 0.0).astype(jnp.bfloat16)
            fresh_acc[c, h] = jnp.dot(
                weights, jnp.concatenate([values, fresh_ones], axis=1), preferred_element_type=jnp.float32
            )

    def combine(c):
        for o in range(c * per_chunk, (c + 1) * per_chunk):
            if o:
                send_r[o].wait_recv()
                send_d[o].wait_recv()
        for i in range(chunk_lanes):
            lane = c * chunk_lanes + i
            o, k = lane // cap, lane % cap
            for h in range(kv_heads):
                for g in range(GROUP):
                    head = GROUP * h + g
                    at = slice(g * chunk_keys + i * rows, g * chunk_keys + (i + 1) * rows)
                    cols = slice(head * HEAD, (head + 1) * HEAD)
                    place = k * q_heads + head
                    den = fresh_acc[c, h, at, HEAD:] + den_in[o, :, place : place + 1]
                    num = fresh_acc[c, h, at, :HEAD] + res_in[lane, :, cols].astype(jnp.float32)
                    att[c, i * rows : (i + 1) * rows, cols] = (num / den).astype(jnp.bfloat16)
        send_a[c].start()

    def project(c):
        send_a[c].wait_recv()
        if c == 0:
            for m in range(halves):
                load_w[m].wait()
                send_w[m].wait_recv()
        for m in range(1, halves):
            part_out[c, m] = jnp.dot(att[c], w[m], preferred_element_type=jnp.float32).astype(jnp.bfloat16)
            send_p[c, m].start()
        own = jnp.dot(att[c], w[0], preferred_element_type=jnp.float32)
        branch[c * chunk_lanes : (c + 1) * chunk_lanes] = own.reshape(chunk_lanes, rows, own_cols)

    def gather_sum(c):
        here = slice(c * chunk_lanes, (c + 1) * chunk_lanes)
        total = branch[here].reshape(chunk_rows, own_cols)
        for m in range(1, halves):
            send_p[c, m].wait_recv()
            total = total + part_in[c, m].astype(jnp.float32)
        branch[here] = total.reshape(chunk_lanes, rows, own_cols)
        squares = jnp.sum(total * total, axis=1, keepdims=True)
        ss_out[c] = jnp.transpose(jnp.broadcast_to(squares, (chunk_rows, chunk_rows)))[:8]
        for u in range(1, tensor_count):
            send_n[c, u].start()

    def answer(o):
        send_i[o].wait_recv()
        spill = pltpu.make_async_copy(idx_in.at[o], idx_smem.at[o], s_sem.at[o])
        spill.start()
        spill.wait()
        send_q[o].wait_recv()
        serve(q_in, o, lambda k: idx_smem[o, 0, k], res_out, den_out)
        send_d[o].start()
        send_r[o].start()

    alone = per_chunk == 1
    serve(ql, 0, lambda k: lists[3 * slots + k], res_in, den_in)
    fresh_part(0)
    if alone:
        combine(0)
        fresh_part(1)
        project(0)
    for c in range(chunks):
        for o in range(c * per_chunk, (c + 1) * per_chunk):
            if o:
                answer(o)
        if c + 1 < chunks and not (alone and c == 0):
            fresh_part(c + 1)
    for c in range(1 if alone else 0, chunks):
        combine(c)
        if c == 1:
            gather_sum(0)
        project(c)
    for c in range(1, chunks):
        gather_sum(c)

    for c in range(chunks):
        squares = ss_out[c]
        for u in range(1, tensor_count):
            send_n[c, u].wait_recv()
            squares = squares + ss_in[c, u]
        wide = jnp.broadcast_to(squares[:1], (chunk_rows, chunk_rows))
        mean_square = jnp.transpose(wide)[:, :1] * (1.0 / model_width)
        here = slice(c * chunk_lanes, (c + 1) * chunk_lanes)
        scale = lax.rsqrt(mean_square + norm_eps)
        normed = branch[here].reshape(chunk_rows, own_cols) * scale * gain[...].reshape(1, own_cols)
        branch[here] = normed.reshape(chunk_lanes, rows, own_cols)

    def to_slot(slot, _):
        out[slot] = branch[lane_of(slot)].astype(jnp.bfloat16)
        return 0

    lax.fori_loop(0, slots, to_slot, 0, unroll=4)

    for o in range(1, dp_count):
        for sent in (send_q[o], send_i[o], send_r[o], send_d[o]):
            sent.wait_send()
    for sent in [*send_w, *send_a, *send_p.values(), *send_n.values()]:
        sent.wait_send()


def shards(kv_cache, lengths, source, queries, fresh_kv, out_weight, norm_gain):
    dp_count = lax.axis_size("dp")
    tensor_count = lax.axis_size("tensor")
    slots, rows, q_width = queries.shape
    kv_width = kv_cache.shape[2]
    kv_heads = kv_width // (2 * HEAD)
    cap = max(1, slots // dp_count)
    model_width = out_weight.shape[1]
    true_cols = norm_gain.shape[0]
    own_cols = -(-true_cols // 128) * 128
    depth = out_weight.shape[0]
    halves = tensor_count // 2
    chunk_lanes = max(cap, slots // 4)
    chunks = slots // chunk_lanes
    chunk_rows = chunk_lanes * rows

    if own_cols != true_cols:
        spare = own_cols - true_cols
        blocks = out_weight.reshape(depth, tensor_count, true_cols).transpose(1, 0, 2)
        out_weight = jnp.pad(blocks, ((0, 0), (0, 0), (0, spare)))
        norm_gain = jnp.pad(norm_gain, (0, spare))

    home = source // slots
    offset = (home - lax.axis_index("dp").astype(jnp.int32) + dp_count) % dp_count
    ids = jnp.arange(slots, dtype=jnp.int32)
    same = (offset[:, None] == offset[None, :]) & (ids[None, :] < ids[:, None])
    lane_of_slot = offset * cap + jnp.sum(same.astype(jnp.int32), axis=1)
    hits = lane_of_slot[None, :] == ids[:, None]
    slot_of_lane = jnp.sum(jnp.where(hits, ids[None, :], 0), axis=1)
    old_slot = jnp.sum(jnp.where(hits, (source % slots)[None, :], 0), axis=1)
    lists = jnp.concatenate([lengths, slot_of_lane, lane_of_slot, old_slot])
    old_slots = jnp.pad(old_slot.reshape(dp_count, 1, cap), ((0, 0), (0, 7), (0, 128 - cap)))

    vmem = pl.BlockSpec(memory_space=pltpu.VMEM)
    hbm = pl.BlockSpec(memory_space=pl.ANY)
    dma = pltpu.SemaphoreType.DMA
    bf16, f32, i32 = jnp.bfloat16, jnp.float32, jnp.int32
    normed = pl.pallas_call(
        functools.partial(kernel, dp_count, tensor_count, cap, model_width),
        out_shape=jax.ShapeDtypeStruct((slots, rows, own_cols), bf16),
        in_specs=[vmem, vmem, hbm, hbm, hbm, hbm, hbm],
        out_specs=vmem,
        scratch_shapes=[
            pltpu.VMEM(kv_cache.shape, bf16),
            pltpu.VMEM(queries.shape, bf16),
            pltpu.VMEM(fresh_kv.shape, bf16),
            pltpu.VMEM((halves, 2 * depth, own_cols), bf16),
            pltpu.VMEM(queries.shape, bf16),
            pltpu.VMEM(fresh_kv.shape, bf16),
            pltpu.VMEM(queries.shape, bf16),
            pltpu.VMEM((dp_count, 8, 128), i32),
            pltpu.SMEM((dp_count, 8, 128), i32),
            pltpu.SMEM((4 * slots,), i32),
            pltpu.VMEM(queries.shape, bf16),
            pltpu.VMEM(queries.shape, bf16),
            pltpu.VMEM((dp_count, rows, 128), f32),
            pltpu.VMEM((dp_count, rows, 128), f32),
            pltpu.VMEM((chunks, kv_heads, GROUP * chunk_rows, 2 * HEAD), f32),
            pltpu.VMEM((chunks, chunk_rows, 2 * q_width), bf16),
            pltpu.VMEM((chunks, halves, chunk_rows, own_cols), bf16),
            pltpu.VMEM((chunks, halves, chunk_rows, own_cols), bf16),
            pltpu.VMEM((slots, rows, own_cols), f32),
            pltpu.VMEM((chunks, 8, 128), f32),
            pltpu.VMEM((chunks, tensor_count, 8, 128), f32),
            dma((3 + halves,)),
            dma((halves,)),
            dma((halves,)),
            *[dma((dp_count,)) for _ in range(9)],
            dma((chunks,)),
            dma((chunks,)),
            dma((chunks, halves)),
            dma((chunks, halves)),
            dma((chunks, tensor_count)),
            dma((chunks, tensor_count)),
        ],
        compiler_params=pltpu.CompilerParams(
            collective_id=0, has_side_effects=True, vmem_limit_bytes=60 * 2**20
        ),
        cost_estimate=pl.CostEstimate(
            flops=2 * slots * rows * depth * own_cols * tensor_count,
            bytes_accessed=2 * (kv_cache.size + out_weight.size),
            transcendentals=0,
        ),
    )(
        old_slots,
        norm_gain,
        lists,
        kv_cache,
        queries,
        fresh_kv,
        out_weight,
    )
    return normed[:, :, :true_cols]


def solution(mesh):
    placed = (
        P(("groups", "dp"), None, "tensor"),
        P(("groups", "dp")),
        P(("groups", "dp")),
        P(("groups", "dp"), None, "tensor"),
        P(("groups", "dp"), None, "tensor"),
        P("tensor", None),
        P("tensor"),
    )
    return jax.shard_map(
        shards,
        mesh=mesh,
        in_specs=placed,
        out_specs=P(("groups", "dp"), None, "tensor"),
        check_vma=False,
    )
```

```python
import functools

import jax
import jax.numpy as jnp
from jax import lax
from jax.experimental import pallas as pl
from jax.experimental.pallas import tpu as pltpu
from jax.sharding import PartitionSpec as P

HEAD = 128
QHEADS = 16
KVHEADS = 8
GROUP = QHEADS // KVHEADS

score_scale = 144.0 ** (-0.5)
soft_cap = 50.0
norm_eps = 1e-06

MESH = pl.DeviceIdType.MESH
NT = (((1,), (1,)), ((), ()))


def capped_exp(scores):
    return jnp.exp(soft_cap * jnp.tanh(scores * (score_scale / soft_cap)))


def kernel(
    dp_count,
    tensor_count,
    cap,
    model_width,
    old_slots,
    gain,
    lists_hbm,
    kv_hbm,
    q_hbm,
    fresh_hbm,
    w_hbm,
    out,
    kv,
    q,
    fresh,
    w,
    ql,
    fl,
    q_in,
    idx_in,
    idx_smem,
    lists,
    res_out,
    res_in,
    den_out,
    den_in,
    fresh_acc,
    att,
    part_out,
    part_in,
    branch,
    ss_out,
    ss_in,
    local_sem,
    w_send,
    w_recv,
    q_send,
    q_recv,
    i_send,
    i_recv,
    s_sem,
    r_send,
    r_recv,
    d_send,
    d_recv,
    a_send,
    a_recv,
    p_send,
    p_recv,
    n_send,
    n_recv,
):
    slots, rows, q_width = q.shape
    cache_len = kv.shape[1]
    kv_heads = kv.shape[2] // (2 * HEAD)
    q_heads = q_width // HEAD
    halves = tensor_count // 2
    own_cols = out.shape[2]
    chunks, chunk_rows, _ = att.shape
    chunk_lanes = slots // chunks
    per_chunk = chunk_lanes // cap
    depth = w_hbm.shape[-2]

    me = lax.axis_index("dp")
    my_t = lax.axis_index("tensor")
    partner = my_t + 1 - 2 * lax.rem(my_t, 2)

    def dp_peer(o):
        return lax.rem(me + o, dp_count)

    def t_peer(u):
        return lax.rem(my_t + u, tensor_count)

    def w_block(block):
        if len(w_hbm.shape) == 3:
            return w_hbm.at[block]
        return w_hbm.at[:, pl.ds(pl.multiple_of(block * own_cols, 128), own_cols)]

    def length_of(slot):
        return lists[slot]

    def slot_of(lane):
        return lists[slots + lane]

    def lane_of(slot):
        return lists[2 * slots + slot]

    load_lists = pltpu.make_async_copy(lists_hbm, lists, s_sem.at[0])
    load_q = pltpu.make_async_copy(q_hbm, q, local_sem.at[0])
    load_fresh = pltpu.make_async_copy(fresh_hbm, fresh, local_sem.at[1])
    load_kv = pltpu.make_async_copy(kv_hbm, kv, local_sem.at[2])
    load_w = [
        pltpu.make_async_copy(
            w_block(t_peer(2 * m)), w.at[m, pl.ds(0, depth)], local_sem.at[3 + m]
        )
        for m in range(halves)
    ]
    load_lists.start()
    load_q.start()
    load_kv.start()
    load_fresh.start()
    for m in range(halves - 1, -1, -1):
        load_w[m].start()

    barrier = pltpu.get_barrier_semaphore()
    for o in range(1, dp_count):
        pl.semaphore_signal(barrier, 1, device_id={"dp": dp_peer(o)}, device_id_type=MESH)
    for u in range(1, tensor_count):
        pl.semaphore_signal(barrier, 1, device_id={"tensor": t_peer(u)}, device_id_type=MESH)
    load_lists.wait()
    load_q.wait()

    def to_lane(lane, _):
        ql[lane] = q[slot_of(lane)]
        return 0

    lax.fori_loop(0, slots, to_lane, 0, unroll=8)
    pl.semaphore_wait(barrier, dp_count - 1 + tensor_count - 1)

    def remote(src, dst, send, recv, where):
        return pltpu.make_async_remote_copy(
            src_ref=src, dst_ref=dst, send_sem=send, recv_sem=recv, device_id=where, device_id_type=MESH
        )

    send_w = [
        remote(
            w_block(lax.rem(partner + 2 * m, tensor_count)),
            w.at[m, pl.ds(depth, depth)],
            w_send.at[m],
            w_recv.at[m],
            {"tensor": partner},
        )
        for m in range(halves)
    ]
    send_q, send_i, send_r, send_d = {}, {}, {}, {}
    for o in range(1, dp_count):
        lanes = pl.ds(o * cap, cap)
        there, back = {"dp": dp_peer(o)}, {"dp": dp_peer(dp_count - o)}
        send_q[o] = remote(ql.at[lanes], q_in.at[lanes], q_send.at[o], q_recv.at[o], there)
        send_i[o] = remote(old_slots.at[o], idx_in.at[o], i_send.at[o], i_recv.at[o], there)
        send_r[o] = remote(res_out.at[lanes], res_in.at[lanes], r_send.at[o], r_recv.at[o], back)
        send_d[o] = remote(den_out.at[o], den_in.at[o], d_send.at[o], d_recv.at[o], back)
    send_a = [
        remote(
            att.at[c, :, pl.ds(0, q_width)],
            att.at[c, :, pl.ds(q_width, q_width)],
            a_send.at[c],
            a_recv.at[c],
            {"tensor": partner},
        )
        for c in range(chunks)
    ]
    send_p = {
        (c, m): remote(
            part_out.at[c, m], part_in.at[c, m], p_send.at[c, m], p_recv.at[c, m], {"tensor": t_peer(2 * m)}
        )
        for c in range(chunks)
        for m in range(1, halves)
    }
    send_n = {
        (c, u): remote(ss_out.at[c], ss_in.at[c, u], n_send.at[c, u], n_recv.at[c, u], {"tensor": t_peer(u)})
        for c in range(chunks)
        for u in range(1, tensor_count)
    }

    for o in range(1, dp_count):
        send_i[o].start()
        send_q[o].start()
    for m in range(halves - 1, -1, -1):
        send_w[m].start()
    load_fresh.wait()

    def fresh_to_lane(lane, _):
        fl[lane] = fresh[slot_of(lane)]
        return 0

    lax.fori_loop(0, slots, fresh_to_lane, 0, unroll=8)
    load_kv.wait()

    column = lax.broadcasted_iota(jnp.int32, (rows, HEAD), 1)
    position = lax.broadcasted_iota(jnp.int32, (GROUP * rows, cache_len), 1)
    ones = jnp.ones((cache_len, HEAD), jnp.bfloat16)

    def serve(q_ref, o, slot_at, res, dens):
        total = jnp.zeros((rows, HEAD), jnp.float32)
        for k in range(cap):
            lane = o * cap + k
            slot = slot_at(k)
            length = length_of(slot)
            for h in range(kv_heads):
                first = GROUP * h * HEAD
                asked = jnp.concatenate(
                    [q_ref[lane, :, first + g * HEAD : first + (g + 1) * HEAD] for g in range(GROUP)], axis=0
                )
                keys = kv[slot, :, 2 * h * HEAD : (2 * h + 1) * HEAD]
                values = kv[slot, :, (2 * h + 1) * HEAD : (2 * h + 2) * HEAD]
                scores = lax.dot_general(asked, keys, NT, preferred_element_type=jnp.float32)
                weights = jnp.where(position < length, capped_exp(scores), 0.0).astype(jnp.bfloat16)
                summed = jnp.dot(
                    weights, jnp.concatenate([values, ones], axis=1), preferred_element_type=jnp.float32
                )
                for g in range(GROUP):
                    part = summed[g * rows : (g + 1) * rows]
                    res[lane, :, first + g * HEAD : first + (g + 1) * HEAD] = part[:, :HEAD].astype(jnp.bfloat16)
                    total = jnp.where(column == k * q_heads + GROUP * h + g, part[:, HEAD:], total)
        dens[o] = total

    chunk_keys = chunk_lanes * rows
    row_id = lax.rem(lax.broadcasted_iota(jnp.int32, (GROUP * chunk_keys, chunk_keys), 0), chunk_keys)
    key_id = lax.broadcasted_iota(jnp.int32, (GROUP * chunk_keys, chunk_keys), 1)
    in_block = (row_id // rows == key_id // rows) & (key_id <= row_id)
    fresh_ones = jnp.ones((chunk_keys, HEAD), jnp.bfloat16)

    def fresh_part(c):
        lanes = slice(c * chunk_lanes, (c + 1) * chunk_lanes)
        for h in range(kv_heads):
            first = GROUP * h * HEAD
            asked = jnp.concatenate(
                [
                    ql[lanes, :, first + g * HEAD : first + (g + 1) * HEAD].reshape(chunk_keys, HEAD)
                    for g in range(GROUP)
                ],
                axis=0,
            )
            keys = fl[lanes, :, 2 * h * HEAD : (2 * h + 1) * HEAD].reshape(chunk_keys, HEAD)
            values = fl[lanes, :, (2 * h + 1) * HEAD : (2 * h + 2) * HEAD].reshape(chunk_keys, HEAD)
            scores = lax.dot_general(asked, keys, NT, preferred_element_type=jnp.float32)
            weights = jnp.where(in_block, capped_exp(scores), 0.0).astype(jnp.bfloat16)
            fresh_acc[c, h] = jnp.dot(
                weights, jnp.concatenate([values, fresh_ones], axis=1), preferred_element_type=jnp.float32
            )

    def combine(c):
        for o in range(c * per_chunk, (c + 1) * per_chunk):
            if o:
                send_r[o].wait_recv()
                send_d[o].wait_recv()
        for i in range(chunk_lanes):
            lane = c * chunk_lanes + i
            o, k = lane // cap, lane % cap
            for h in range(kv_heads):
                for g in range(GROUP):
                    head = GROUP * h + g
                    at = slice(g * chunk_keys + i * rows, g * chunk_keys + (i + 1) * rows)
                    cols = slice(head * HEAD, (head + 1) * HEAD)
                    place = k * q_heads + head
                    den = fresh_acc[c, h, at, HEAD:] + den_in[o, :, place : place + 1]
                    num = fresh_acc[c, h, at, :HEAD] + res_in[lane, :, cols].astype(jnp.float32)
                    att[c, i * rows : (i + 1) * rows, cols] = (num / den).astype(jnp.bfloat16)
        send_a[c].start()

    def project(c):
        send_a[c].wait_recv()
        for m in range(1, halves):
            if c == 0:
                load_w[m].wait()
                send_w[m].wait_recv()
            part_out[c, m] = jnp.dot(att[c], w[m], preferred_element_type=jnp.float32).astype(jnp.bfloat16)
            send_p[c, m].start()

    def project_own(c):
        if c == 0:
            load_w[0].wait()
            send_w[0].wait_recv()
        own = jnp.dot(att[c], w[0], preferred_element_type=jnp.float32)
        branch[c * chunk_lanes : (c + 1) * chunk_lanes] = own.reshape(chunk_lanes, rows, own_cols)

    def gather_sum(c):
        here = slice(c * chunk_lanes, (c + 1) * chunk_lanes)
        total = branch[here].reshape(chunk_rows, own_cols)
        for m in range(1, halves):
            send_p[c, m].wait_recv()
            total = total + part_in[c, m].astype(jnp.float32)
        branch[here] = total.reshape(chunk_lanes, rows, own_cols)
        squares = jnp.sum(total * total, axis=1, keepdims=True)
        ss_out[c] = jnp.transpose(jnp.broadcast_to(squares, (chunk_rows, chunk_rows)))[:8]
        for u in range(1, tensor_count):
            send_n[c, u].start()

    def answer(o):
        send_i[o].wait_recv()
        spill = pltpu.make_async_copy(idx_in.at[o], idx_smem.at[o], s_sem.at[o])
        spill.start()
        spill.wait()
        send_q[o].wait_recv()
        serve(q_in, o, lambda k: idx_smem[o, 0, k], res_out, den_out)
        send_d[o].start()
        send_r[o].start()

    alone = per_chunk == 1
    serve(ql, 0, lambda k: lists[3 * slots + k], res_in, den_in)
    fresh_part(0)
    if alone:
        combine(0)
        answer(1)
        fresh_part(1)
        project(0)
        for o in range(2, dp_count):
            answer(o)
        project_own(0)
        for c in range(2, chunks):
            fresh_part(c)
    else:
        for o in range(1, dp_count):
            answer(o)
        for c in range(1, chunks):
            fresh_part(c)
    for c in range(1 if alone else 0, chunks):
        combine(c)
        project(c)
        project_own(c)
        if c == 1:
            gather_sum(0)
    for c in range(1, chunks):
        gather_sum(c)

    for c in range(chunks):
        squares = ss_out[c]
        for u in range(1, tensor_count):
            send_n[c, u].wait_recv()
            squares = squares + ss_in[c, u]
        wide = jnp.broadcast_to(squares[:1], (chunk_rows, chunk_rows))
        mean_square = jnp.transpose(wide)[:, :1] * (1.0 / model_width)
        here = slice(c * chunk_lanes, (c + 1) * chunk_lanes)
        scale = lax.rsqrt(mean_square + norm_eps)
        normed = branch[here].reshape(chunk_rows, own_cols) * scale * gain[...].reshape(1, own_cols)
        branch[here] = normed.reshape(chunk_lanes, rows, own_cols)

    def to_slot(slot, _):
        out[slot] = branch[lane_of(slot)].astype(jnp.bfloat16)
        return 0

    lax.fori_loop(0, slots, to_slot, 0, unroll=4)

    for o in range(1, dp_count):
        for sent in (send_q[o], send_i[o], send_r[o], send_d[o]):
            sent.wait_send()
    for sent in [*send_w, *send_a, *send_p.values(), *send_n.values()]:
        sent.wait_send()


def shards(kv_cache, lengths, source, queries, fresh_kv, out_weight, norm_gain):
    dp_count = lax.axis_size("dp")
    tensor_count = lax.axis_size("tensor")
    slots, rows, q_width = queries.shape
    kv_width = kv_cache.shape[2]
    kv_heads = kv_width // (2 * HEAD)
    cap = max(1, slots // dp_count)
    model_width = out_weight.shape[1]
    true_cols = norm_gain.shape[0]
    own_cols = -(-true_cols // 128) * 128
    depth = out_weight.shape[0]
    halves = tensor_count // 2
    chunk_lanes = max(cap, slots // 4)
    chunks = slots // chunk_lanes
    chunk_rows = chunk_lanes * rows

    if own_cols != true_cols:
        spare = own_cols - true_cols
        blocks = out_weight.reshape(depth, tensor_count, true_cols).transpose(1, 0, 2)
        out_weight = jnp.pad(blocks, ((0, 0), (0, 0), (0, spare)))
        norm_gain = jnp.pad(norm_gain, (0, spare))

    home = source // slots
    offset = (home - lax.axis_index("dp").astype(jnp.int32) + dp_count) % dp_count
    ids = jnp.arange(slots, dtype=jnp.int32)
    same = (offset[:, None] == offset[None, :]) & (ids[None, :] < ids[:, None])
    lane_of_slot = offset * cap + jnp.sum(same.astype(jnp.int32), axis=1)
    hits = lane_of_slot[None, :] == ids[:, None]
    slot_of_lane = jnp.sum(jnp.where(hits, ids[None, :], 0), axis=1)
    old_slot = jnp.sum(jnp.where(hits, (source % slots)[None, :], 0), axis=1)
    lists = jnp.concatenate([lengths, slot_of_lane, lane_of_slot, old_slot])
    old_slots = jnp.pad(old_slot.reshape(dp_count, 1, cap), ((0, 0), (0, 7), (0, 128 - cap)))

    vmem = pl.BlockSpec(memory_space=pltpu.VMEM)
    hbm = pl.BlockSpec(memory_space=pl.ANY)
    dma = pltpu.SemaphoreType.DMA
    bf16, f32, i32 = jnp.bfloat16, jnp.float32, jnp.int32
    normed = pl.pallas_call(
        functools.partial(kernel, dp_count, tensor_count, cap, model_width),
        out_shape=jax.ShapeDtypeStruct((slots, rows, own_cols), bf16),
        in_specs=[vmem, vmem, hbm, hbm, hbm, hbm, hbm],
        out_specs=vmem,
        scratch_shapes=[
            pltpu.VMEM(kv_cache.shape, bf16),
            pltpu.VMEM(queries.shape, bf16),
            pltpu.VMEM(fresh_kv.shape, bf16),
            pltpu.VMEM((halves, 2 * depth, own_cols), bf16),
            pltpu.VMEM(queries.shape, bf16),
            pltpu.VMEM(fresh_kv.shape, bf16),
            pltpu.VMEM(queries.shape, bf16),
            pltpu.VMEM((dp_count, 8, 128), i32),
            pltpu.SMEM((dp_count, 8, 128), i32),
            pltpu.SMEM((4 * slots,), i32),
            pltpu.VMEM(queries.shape, bf16),
            pltpu.VMEM(queries.shape, bf16),
            pltpu.VMEM((dp_count, rows, 128), f32),
            pltpu.VMEM((dp_count, rows, 128), f32),
            pltpu.VMEM((chunks, kv_heads, GROUP * chunk_rows, 2 * HEAD), f32),
            pltpu.VMEM((chunks, chunk_rows, 2 * q_width), bf16),
            pltpu.VMEM((chunks, halves, chunk_rows, own_cols), bf16),
            pltpu.VMEM((chunks, halves, chunk_rows, own_cols), bf16),
            pltpu.VMEM((slots, rows, own_cols), f32),
            pltpu.VMEM((chunks, 8, 128), f32),
            pltpu.VMEM((chunks, tensor_count, 8, 128), f32),
            dma((3 + halves,)),
            dma((halves,)),
            dma((halves,)),
            *[dma((dp_count,)) for _ in range(9)],
            dma((chunks,)),
            dma((chunks,)),
            dma((chunks, halves)),
            dma((chunks, halves)),
            dma((chunks, tensor_count)),
            dma((chunks, tensor_count)),
        ],
        compiler_params=pltpu.CompilerParams(
            collective_id=0, has_side_effects=True, vmem_limit_bytes=48 * 2**20
        ),
        cost_estimate=pl.CostEstimate(
            flops=2 * slots * rows * depth * own_cols * tensor_count,
            bytes_accessed=2 * (kv_cache.size + out_weight.size),
            transcendentals=0,
        ),
    )(
        old_slots,
        norm_gain,
        lists,
        kv_cache,
        queries,
        fresh_kv,
        out_weight,
    )
    return normed[:, :, :true_cols]


def solution(mesh):
    placed = (
        P(("groups", "dp"), None, "tensor"),
        P(("groups", "dp")),
        P(("groups", "dp")),
        P(("groups", "dp"), None, "tensor"),
        P(("groups", "dp"), None, "tensor"),
        P("tensor", None),
        P("tensor"),
    )
    return jax.shard_map(
        shards,
        mesh=mesh,
        in_specs=placed,
        out_specs=P(("groups", "dp"), None, "tensor"),
        check_vma=False,
    )
```
